32 devices in a mesh: groups: 2 (over y), tensor: 4 (over x, core), dp: 4 (over z).
Axes of the slice: x: 2, y: 2, z: 4, core: 2. Of those that a mesh axis runs over, the one named last changes fastest.
Arguments:
- activations: bfloat16 [16384, 28672], P(('groups', 'dp'), 'tensor'), parts along dimension 0, may hold values from -6 to 6
- out_grads: bfloat16 [16384, 8192], P(('groups', 'dp'), 'tensor'), parts along dimension 0, may hold values from -6 to 6
- proj_in: bfloat16 [57344, 32], P(('groups', 'tensor')), parts along dimension 0, may hold values from -0.03125 to 0.03125
- proj_out: bfloat16 [16384, 32], P(('groups', 'tensor')), parts along dimension 0, may hold values from -0.0625 to 0.0625
- document_ids: int32 [8, 2048], P(('groups', 'dp')), parts along dimension 0, may hold values from 0 to 31, never falling along the last dimension, each value on 1 to 128 neighbouring positions
Outputs:
- sketches: float32 [256, 1024], P(('groups', 'dp'), 'tensor'), parts along dimension 0
- fisher: float32 [2048, 1024], P(('groups', 'dp'), 'tensor'), parts along dimension 0
The draws below stay inside these ranges and needn't reach their ends.
There are 2 independent parts, one for each index of `groups`. The reference program is written for one: setup_inputs(seed, part) draws one part's arguments, and reference() takes and returns one part's arrays. A program takes and returns all parts, laid end to end along the dimension named above; each array names one. Nothing has to cross between parts.
Inputs may be any that keep to these rules, and one draw needn't show every extreme that they name: `document_ids`: each row never falls; each of its 32 documents has 1 to 128 tokens, one exactly 128.
All inputs are finite; a program needn't handle non-finite values.
Results may differ from the reference program's by a relative error of at most 0.0003.
Values sent between devices are 32-bit elements; how exact they have to be, the bound alone decides.
A program may use at most 128 MiB of HBM per device.

```python
import math
import jax
import jax.numpy as jnp
import numpy as np
from jax import lax

D = 8192
FF = 28672
RANK = 32
TOK_DEV = 2048
DOCS_DEV = 32
MOST = 128
TOKENS = 8192
DOCS = 128
N_DP = 4


def levels(stream_key, shape, shards, low, top_value):
    level = 1.0
    for position, shards_of in shards:
        heights = jax.random.uniform(jax.random.fold_in(jax.random.fold_in(stream_key, 6), position), (shards_of,), jnp.float32, low / len(shards), top_value / len(shards))
        level = level * jnp.repeat(jnp.exp(heights), shape[position] // shards_of).reshape((-1,) + (1,) * (len(shape) - 1 - position))
    return level


def profile(number_of, total, limit, lean):
    portions = [(1 << 20) // math.isqrt(grade ** lean) + 1 for grade in range(2, number_of + 1)]
    spare, given = total - limit - (number_of - 1), [1] * (number_of - 1)
    while spare > 0:
        free = [i for i in range(number_of - 1) if given[i] < limit]
        whole, remaining = sum([portions[i] for i in free]), spare
        for i in free:
            addition = min(limit - given[i], max(1, remaining * portions[i] // whole), spare)
            given[i] = given[i] + addition
            spare = spare - addition
    return np.array([limit] + given)


def ragged_sizes(rng, count, total, bound, skew):
    if count == 2:
        one = jax.random.randint(rng, (), max(1, total - bound), min(bound, total - 1) + 1)
        return jnp.stack([one, total - one])
    sizes = jnp.asarray(profile(count, total, bound, skew), jnp.int32)
    twos = (count - 1) // 2
    donor, receiver = sizes[1:1 + 2 * twos:2], sizes[2:2 + 2 * twos:2]
    room = jnp.minimum(donor - 1, bound - receiver)
    passed = jax.random.randint(jax.random.fold_in(rng, 1), (twos,), 0, 1 << 20) % (room + 1)
    sizes = sizes.at[1:1 + 2 * twos:2].set(donor - passed).at[2:2 + 2 * twos:2].set(receiver + passed)
    return sizes[jax.random.permutation(jax.random.fold_in(rng, 2), count)]


def bell_draw(stream_key, shape, scale, reach, pieces=(), kind=jnp.bfloat16):
    array = jax.random.normal(stream_key, shape, jnp.float32) * scale
    if len(pieces) > 0:
        array = levels(stream_key, shape, pieces, -0.22, 0.18) * array
    return jnp.clip(array, min=-reach, max=reach).astype(kind)


def setup_inputs(seed: int = 0, part: int = 0) -> dict:
    keys = jax.random.split(jax.random.key(seed), 6)
    part_splits = jax.random.split(jax.random.fold_in(keys[5], part), 6)
    return {
        "activations": bell_draw(part_splits[0], (TOKENS, FF), 1.0, 6.0, ((0, 4), (1, 4))),
        "out_grads": bell_draw(part_splits[1], (TOKENS, D), 1.0, 6.0, ((0, 4), (1, 4))),
        "proj_in": bell_draw(part_splits[2], (FF, RANK), FF ** -0.5, 0.03125, ((0, 4),)),
        "proj_out": bell_draw(part_splits[3], (D, RANK), D ** -0.5, 0.0625, ((0, 4),)),
        "document_ids": jax.vmap(lambda own: jnp.searchsorted(jnp.cumsum(ragged_sizes(own, DOCS_DEV, TOK_DEV, MOST, 2)), jnp.arange(TOK_DEV), side="right"))(jax.random.split(part_splits[4], N_DP)).reshape((N_DP, TOK_DEV)).astype(jnp.int32),
    }


def reference(activations, out_grads, proj_in, proj_out, document_ids):
    in_proj = jnp.dot(activations, proj_in, preferred_element_type=jnp.float32)
    out_proj = jnp.dot(out_grads, proj_out, preferred_element_type=jnp.float32)
    offsets = (jnp.arange(N_DP, dtype=jnp.int32) * DOCS_DEV)[:, None]
    global_ids = (document_ids + offsets).reshape(-1)
    onehot = (global_ids[:, None] == jnp.arange(DOCS, dtype=jnp.int32)[None, :]).astype(jnp.float32)
    length = lax.optimization_barrier(jnp.sum(onehot, axis=0))
    weighted = onehot * lax.rsqrt(length)[None, :]
    outer_rows = (out_proj[:, :, None] * in_proj[:, None, :]).reshape(TOKENS, RANK * RANK)
    sketches = jnp.dot(weighted.T, outer_rows, precision=lax.Precision.HIGHEST)
    fisher = jnp.dot(sketches.T, sketches, precision=lax.Precision.HIGHEST) / DOCS
    return (sketches, fisher)
```

```python
import jax
import jax.numpy as jnp
from jax import lax
from jax.experimental import pallas as pl
from jax.experimental.pallas import tpu as pltpu
from jax.sharding import PartitionSpec as P

DOCS_DEV = 32
MESH = pl.DeviceIdType.MESH
F32 = jnp.float32
BF16 = jnp.bfloat16


def sketch_terms(in_proj, out_proj, weighted):
    token_count = in_proj.shape[0]
    rank_size = in_proj.shape[1]
    outer_rows = (out_proj[:, :, None] * in_proj[:, None, :]).reshape(
        token_count, rank_size * rank_size
    )
    return jnp.dot(weighted.T, outer_rows, precision=lax.Precision.HIGHEST)


def per_device_general(activations, out_grads, proj_in, proj_out, document_ids):
    in_part = jnp.dot(activations, proj_in, preferred_element_type=F32)
    out_part = jnp.dot(out_grads, proj_out, preferred_element_type=F32)
    onehot = (document_ids[0][:, None] == jnp.arange(DOCS_DEV, dtype=jnp.int32)[None, :]).astype(F32)
    length = jnp.sum(onehot, axis=0)
    weighted = onehot * lax.rsqrt(length)[None, :]
    tensor_count = lax.axis_size("tensor")
    tensor_index = lax.axis_index("tensor")
    sketch_size = proj_in.shape[1] * proj_in.shape[1]
    col_count = sketch_size // tensor_count
    in_proj, out_proj = lax.psum((in_part, out_part), "tensor")
    full_sketch = sketch_terms(in_proj, out_proj, weighted)
    own_sketch = lax.dynamic_slice_in_dim(full_sketch, tensor_index * col_count, col_count, 1)
    dp_count = lax.axis_size("dp")
    block_rows = sketch_size // dp_count
    row_first = lax.axis_index("dp") * block_rows
    rows_piece = lax.dynamic_slice_in_dim(
        lax.all_gather(full_sketch, "dp", axis=0, tiled=True), row_first, block_rows, 1
    )
    cols_piece = lax.all_gather(own_sketch, "dp", axis=0, tiled=True)
    fisher = jnp.dot(rows_piece.T, cols_piece, precision=lax.Precision.HIGHEST)
    return (own_sketch, fisher / (DOCS_DEV * dp_count))


N = 4
TB = 256
RANK = 32
OWN = RANK // N


def split(x):
    hi = x.astype(BF16)
    return hi, (x - hi.astype(F32)).astype(BF16)


def kernel(
    act_hbm, grad_hbm, pin_ref, pout_ref, ids_ref, sketch_ref, fisher_ref,
    act, grad, part, sib, mine, send, recv, acc, scol, srow,
    act_sem, grad_sem, sib_send, sib_recv, x_send, x_recv,
    col_send, col_recv, row_send, row_recv,
):
    q = lax.axis_index("tensor")
    z = lax.axis_index("dp")
    blocks = act.shape[0]
    core_peer = q + 1 - 2 * lax.rem(q, 2)
    chip_peer = lax.rem(q + 2, N)

    def load(b):
        rows = pl.ds(pl.multiple_of(b * TB, TB), TB)
        return (
            pltpu.make_async_copy(act_hbm.at[rows], act.at[b], act_sem.at[b]),
            pltpu.make_async_copy(grad_hbm.at[rows], grad.at[b], grad_sem.at[b]),
        )

    def to_core(b):
        return pltpu.make_async_remote_copy(
            src_ref=part.at[b], dst_ref=sib.at[b], send_sem=sib_send.at[b], recv_sem=sib_recv.at[b],
            device_id={"tensor": core_peer}, device_id_type=MESH,
        )

    def to_chip(b):
        return pltpu.make_async_remote_copy(
            src_ref=send.at[b], dst_ref=recv.at[b], send_sem=x_send.at[b], recv_sem=x_recv.at[b],
            device_id={"tensor": chip_peer}, device_id_type=MESH,
        )

    @pl.loop(0, blocks)
    def _(b):
        for copy in load(b):
            copy.start()

    barrier = pltpu.get_barrier_semaphore()
    for dq in range(N):
        for dz in range(N):
            if dq or dz:
                pl.semaphore_signal(
                    barrier, inc=1,
                    device_id={"tensor": lax.rem(q + dq, N), "dp": lax.rem(z + dz, N)},
                    device_id_type=MESH,
                )

    acc[...] = jnp.zeros_like(acc)
    docs = lax.broadcasted_iota(jnp.int32, (DOCS_DEV, 1), 0)
    length = jnp.zeros((DOCS_DEV, 1), F32)
    for b in range(blocks):
        same = (ids_ref[b] == docs).astype(F32)
        length = length + jnp.sum(same, axis=1, keepdims=True)
    scale = lax.rsqrt(length)
    pl.semaphore_wait(barrier, N * N - 1)

    def project(b):
        for copy in load(b):
            copy.wait()
        p_in = jnp.dot(act[b], pin_ref[...], preferred_element_type=F32)
        p_out = jnp.dot(grad[b], pout_ref[...], preferred_element_type=F32)
        part[b, pl.ds(0, RANK)] = p_in.T
        part[b, pl.ds(RANK, RANK)] = p_out.T
        to_core(b).start()

    def chip_sum(b):
        to_core(b).wait()
        total = part[b, pl.ds(0, RANK)] + sib[b, pl.ds(0, RANK)]
        mine[b, pl.ds(0, RANK)] = total
        send[b, pl.ds(0, RANK)] = total
        here = pl.ds(pl.multiple_of(RANK + q * OWN, OWN), OWN)
        there = pl.ds(pl.multiple_of(RANK + chip_peer * OWN, OWN), OWN)
        mine[b, pl.ds(RANK, OWN)] = part[b, here] + sib[b, here]
        send[b, pl.ds(RANK, OWN)] = part[b, there] + sib[b, there]
        to_chip(b).start()

    def sketch(b):
        to_chip(b).wait()
        total = mine[b] + recv[b]
        in_hi, in_lo = split(total[:RANK])
        rhs = jnp.concatenate([in_hi, in_lo], axis=0)
        same = (ids_ref[b] == docs).astype(F32)
        out = total[RANK:]
        out_hi = out.astype(BF16).astype(F32)
        out_lo = out - out_hi
        rows = [same * o[i : i + 1] for o in (out_hi, out_lo) for i in range(OWN)]
        lhs = jnp.concatenate(rows, axis=0).astype(BF16)
        acc[...] += lax.dot_general(
            lhs, rhs, (((1,), (1,)), ((), ())), preferred_element_type=F32
        )

    project(0)
    project(1)
    chip_sum(0)

    @pl.loop(2, blocks)
    def _(b):
        project(b)
        chip_sum(b - 1)
        sketch(b - 2)

    chip_sum(blocks - 1)
    sketch(blocks - 2)
    sketch(blocks - 1)

    half = OWN * DOCS_DEV
    for i in range(OWN):
        hi = acc[pl.ds(i * DOCS_DEV, DOCS_DEV)]
        lo = acc[pl.ds(half + i * DOCS_DEV, DOCS_DEV)]
        both = hi + lo
        piece = (both[:, :RANK] + both[:, RANK:]) * scale
        scol[z, :, pl.ds(i * RANK, RANK)] = piece

    def col_copy(d):
        return pltpu.make_async_remote_copy(
            src_ref=scol.at[z], dst_ref=scol.at[z], send_sem=col_send.at[d], recv_sem=col_recv.at[d],
            device_id={"dp": lax.rem(z + d + 1, N)}, device_id_type=MESH,
        )

    def row_copy(d):
        return pltpu.make_async_remote_copy(
            src_ref=scol.at[z], dst_ref=srow.at[z], send_sem=row_send.at[d], recv_sem=row_recv.at[z],
            device_id={"tensor": lax.rem(q + d + 1, N), "dp": q}, device_id_type=MESH,
        )

    for d in range(N - 1):
        row_copy(d).start()
        col_copy(d).start()
    sketch_ref[...] = scol[z]
    for d in range(N - 1):
        pltpu.make_async_remote_copy(
            src_ref=scol.at[z], dst_ref=scol.at[lax.rem(z + N - d - 1, N)],
            send_sem=col_send.at[d], recv_sem=col_recv.at[d],
            device_id={"dp": lax.rem(z + d + 1, N)}, device_id_type=MESH,
        ).wait_recv()

    @pl.when(q != z)
    def _():
        for d in range(N):
            pltpu.make_async_remote_copy(
                src_ref=scol.at[z], dst_ref=srow.at[d],
                send_sem=row_send.at[0], recv_sem=row_recv.at[d],
                device_id={"tensor": lax.rem(q + 1, N), "dp": q}, device_id_type=MESH,
            ).wait_recv()

    @pl.when(q == z)
    def _():
        srow[...] = scol[...]

    width = OWN * RANK
    col_hi, col_lo = split(scol[...].reshape(N * DOCS_DEV, width))
    row_t = srow[...].reshape(N * DOCS_DEV, width).T
    row_hi, row_lo = split(row_t)
    lhs = jnp.concatenate([row_hi, row_lo, row_hi], axis=1)
    rhs = jnp.concatenate([col_hi, col_hi, col_lo], axis=0)
    fisher_ref[...] = jnp.dot(lhs, rhs, preferred_element_type=F32) * (1.0 / (N * DOCS_DEV))
    for d in range(N - 1):
        row_copy(d).wait_send()
        col_copy(d).wait_send()


def per_device_fused(activations, out_grads, proj_in, proj_out, document_ids):
    tokens, ff = activations.shape
    width = out_grads.shape[1]
    blocks = tokens // TB
    ids = document_ids.reshape(blocks, 1, TB)
    vmem = pl.BlockSpec(memory_space=pltpu.VMEM)
    hbm = pl.BlockSpec(memory_space=pl.ANY)
    cols = OWN * RANK
    dma = pltpu.SemaphoreType.DMA
    return pl.pallas_call(
        kernel,
        out_shape=(
            jax.ShapeDtypeStruct((DOCS_DEV, cols), F32),
            jax.ShapeDtypeStruct((cols, cols), F32),
        ),
        in_specs=[hbm, hbm, vmem, vmem, vmem],
        out_specs=(vmem, vmem),
        scratch_shapes=[
            pltpu.VMEM((blocks, TB, ff), BF16),
            pltpu.VMEM((blocks, TB, width), BF16),
            pltpu.VMEM((blocks, 2 * RANK, TB), F32),
            pltpu.VMEM((blocks, 2 * RANK, TB), F32),
            pltpu.VMEM((blocks, RANK + OWN, TB), F32),
            pltpu.VMEM((blocks, RANK + OWN, TB), F32),
            pltpu.VMEM((blocks, RANK + OWN, TB), F32),
            pltpu.VMEM((2 * OWN * DOCS_DEV, 2 * RANK), F32),
            pltpu.VMEM((N, DOCS_DEV, cols), F32),
            pltpu.VMEM((N, DOCS_DEV, cols), F32),
            dma((blocks,)), dma((blocks,)), dma((blocks,)), dma((blocks,)),
            dma((blocks,)), dma((blocks,)),
            dma((N - 1,)), dma((N - 1,)), dma((N - 1,)), dma((N,)),
        ],
        compiler_params=pltpu.CompilerParams(
            collective_id=0, has_side_effects=True, vmem_limit_bytes=56 * 1024 * 1024
        ),
        cost_estimate=pl.CostEstimate(
            flops=2 * tokens * (ff + width) * RANK,
            bytes_accessed=2 * tokens * (ff + width), transcendentals=0,
        ),
    )(activations, out_grads, proj_in, proj_out, ids)


def solution(mesh):
    fits = mesh.shape["tensor"] == N and mesh.shape["dp"] == N
    return jax.shard_map(
        per_device_fused if fits else per_device_general,
        mesh=mesh,
        in_specs=(
            P(("groups", "dp"), "tensor"),
            P(("groups", "dp"), "tensor"),
            P(("groups", "tensor"), None),
            P(("groups", "tensor"), None),
            P(("groups", "dp"), None),
        ),
        out_specs=(P(("groups", "dp"), "tensor"), P(("groups", "dp"), "tensor")),
        check_vma=False,
    )
```

```python
import jax
import jax.numpy as jnp
from jax import lax
from jax.experimental import pallas as pl
from jax.experimental.pallas import tpu as pltpu
from jax.sharding import PartitionSpec as P

DOCS_DEV = 32
MESH = pl.DeviceIdType.MESH
F32 = jnp.float32
BF16 = jnp.bfloat16


def sketch_terms(in_proj, out_proj, weighted):
    token_count = in_proj.shape[0]
    rank_size = in_proj.shape[1]
    outer_rows = (out_proj[:, :, None] * in_proj[:, None, :]).reshape(
        token_count, rank_size * rank_size
    )
    return jnp.dot(weighted.T, outer_rows, precision=lax.Precision.HIGHEST)


def per_device_general(activations, out_grads, proj_in, proj_out, document_ids):
    in_part = jnp.dot(activations, proj_in, preferred_element_type=F32)
    out_part = jnp.dot(out_grads, proj_out, preferred_element_type=F32)
    onehot = (document_ids[0][:, None] == jnp.arange(DOCS_DEV, dtype=jnp.int32)[None, :]).astype(F32)
    length = jnp.sum(onehot, axis=0)
    weighted = onehot * lax.rsqrt(length)[None, :]
    tensor_count = lax.axis_size("tensor")
    tensor_index = lax.axis_index("tensor")
    sketch_size = proj_in.shape[1] * proj_in.shape[1]
    col_count = sketch_size // tensor_count
    in_proj, out_proj = lax.psum((in_part, out_part), "tensor")
    full_sketch = sketch_terms(in_proj, out_proj, weighted)
    own_sketch = lax.dynamic_slice_in_dim(full_sketch, tensor_index * col_count, col_count, 1)
    dp_count = lax.axis_size("dp")
    block_rows = sketch_size // dp_count
    row_first = lax.axis_index("dp") * block_rows
    rows_piece = lax.dynamic_slice_in_dim(
        lax.all_gather(full_sketch, "dp", axis=0, tiled=True), row_first, block_rows, 1
    )
    cols_piece = lax.all_gather(own_sketch, "dp", axis=0, tiled=True)
    fisher = jnp.dot(rows_piece.T, cols_piece, precision=lax.Precision.HIGHEST)
    return (own_sketch, fisher / (DOCS_DEV * dp_count))


N = 4
TB = 256
RANK = 32
OWN = RANK // N


def split(x):
    hi = x.astype(BF16)
    return hi, (x - hi.astype(F32)).astype(BF16)


def across(a, b):
    return lax.dot_general(a, b, (((1,), (1,)), ((), ())), preferred_element_type=F32)


def kernel(
    act_hbm, grad_hbm, pin_hbm, pout_hbm, ids_ref, scol, srow,
    act, grad, pin_ref, pout_ref, part, sib, mine, send, recv, acc, count, own,
    act_sem, grad_sem, proj_sem, sib_send, sib_recv, x_send, x_recv,
    own_sem, col_send, col_recv, row_send, row_recv,
):
    q = lax.axis_index("tensor")
    z = lax.axis_index("dp")
    blocks = act.shape[0]
    core_peer = q + 1 - 2 * lax.rem(q, 2)
    chip_peer = lax.rem(q + 2, N)

    def load(b):
        rows = pl.ds(pl.multiple_of(b * TB, TB), TB)
        return (
            pltpu.make_async_copy(grad_hbm.at[rows], grad.at[b], grad_sem.at[b]),
            pltpu.make_async_copy(act_hbm.at[rows], act.at[b], act_sem.at[b]),
        )

    def to_core(b):
        return pltpu.make_async_remote_copy(
            src_ref=part.at[b], dst_ref=sib.at[b], send_sem=sib_send.at[b], recv_sem=sib_recv.at[b],
            device_id={"tensor": core_peer}, device_id_type=MESH,
        )

    def to_chip(b):
        return pltpu.make_async_remote_copy(
            src_ref=send.at[b], dst_ref=recv.at[b], send_sem=x_send.at[b], recv_sem=x_recv.at[b],
            device_id={"tensor": chip_peer}, device_id_type=MESH,
        )

    proj_copies = (
        pltpu.make_async_copy(pout_hbm, pout_ref, proj_sem.at[0]),
        pltpu.make_async_copy(pin_hbm, pin_ref, proj_sem.at[1]),
    )
    for copy in proj_copies:
        copy.start()

    @pl.loop(0, blocks)
    def _(b):
        for copy in load(b):
            copy.start()

    barrier = pltpu.get_barrier_semaphore()
    for dq in range(N):
        for dz in range(N):
            if dq or dz:
                pl.semaphore_signal(
                    barrier, inc=1,
                    device_id={"tensor": lax.rem(q + dq, N), "dp": lax.rem(z + dz, N)},
                    device_id_type=MESH,
                )

    acc[...] = jnp.zeros_like(acc)
    docs = lax.broadcasted_iota(jnp.int32, (DOCS_DEV, 1), 0)
    count[...] = jnp.zeros_like(count)

    def project(b):
        grad_copy, act_copy = load(b)
        grad_copy.wait()
        act_copy.wait()
        part[b, pl.ds(RANK, RANK)] = across(pout_ref[...], grad[b])
        part[b, pl.ds(0, RANK)] = across(pin_ref[...], act[b])

        @pl.when(b == 0)
        def _():
            pl.semaphore_wait(barrier, N * N - 1)

        to_core(b).start()

    def chip_sum(b):
        to_core(b).wait()
        total = part[b, pl.ds(0, RANK)] + sib[b, pl.ds(0, RANK)]
        mine[b, pl.ds(0, RANK)] = total
        send[b, pl.ds(0, RANK)] = total
        here = pl.ds(pl.multiple_of(RANK + q * OWN, OWN), OWN)
        there = pl.ds(pl.multiple_of(RANK + chip_peer * OWN, OWN), OWN)
        mine[b, pl.ds(RANK, OWN)] = part[b, here] + sib[b, here]
        send[b, pl.ds(RANK, OWN)] = part[b, there] + sib[b, there]
        to_chip(b).start()

    def sketch(b):
        to_chip(b).wait()
        total = mine[b] + recv[b]
        in_hi, in_lo = split(total[:RANK])
        rhs = jnp.concatenate([in_hi, in_lo], axis=0)
        same = (ids_ref[b] == docs).astype(F32)
        count[...] += same
        out = total[RANK:]
        out_hi = out.astype(BF16).astype(F32)
        out_lo = out - out_hi
        rows = [same * o[i : i + 1] for o in (out_hi, out_lo) for i in range(OWN)]
        lhs = jnp.concatenate(rows, axis=0).astype(BF16)
        acc[...] += across(lhs, rhs)

    for copy in proj_copies:
        copy.wait()

    @pl.loop(0, blocks + 2)
    def _(b):
        pl.when(b < blocks)(lambda: project(b))
        pl.when((b > 0) & (b <= blocks))(lambda: chip_sum(b - 1))
        pl.when(b > 1)(lambda: sketch(b - 2))

    scale = lax.rsqrt(jnp.sum(count[...], axis=1, keepdims=True))
    half = OWN * DOCS_DEV
    for i in range(OWN):
        hi = acc[pl.ds(i * DOCS_DEV, DOCS_DEV)]
        lo = acc[pl.ds(half + i * DOCS_DEV, DOCS_DEV)]
        both = hi + lo
        piece = (both[:, :RANK] + both[:, RANK:]) * scale
        own[:, pl.ds(i * RANK, RANK)] = piece

    def keep():
        return pltpu.make_async_copy(own, scol.at[z], own_sem)

    def col_copy(d, slot):
        return pltpu.make_async_remote_copy(
            src_ref=own, dst_ref=scol.at[slot], send_sem=col_send.at[d], recv_sem=col_recv.at[d],
            device_id={"dp": lax.rem(z + d + 1, N)}, device_id_type=MESH,
        )

    def row_copy(d, slot):
        return pltpu.make_async_remote_copy(
            src_ref=own, dst_ref=srow.at[slot], send_sem=row_send.at[d], recv_sem=row_recv.at[slot],
            device_id={"tensor": lax.rem(q + d + 1, N), "dp": q}, device_id_type=MESH,
        )

    for d in range(N - 1):
        row_copy(d, z).start()
        col_copy(d, z).start()
    keep().start()
    keep().wait()
    for d in range(N - 1):
        col_copy(d, lax.rem(z + N - d - 1, N)).wait_recv()

    @pl.when(q != z)
    def _():
        for d in range(N):
            row_copy(0, d).wait_recv()

    for d in range(N - 1):
        row_copy(d, z).wait_send()
        col_copy(d, z).wait_send()


def fisher_kernel(col_ref, row_ref, sketch_ref, fisher_ref):
    q = lax.axis_index("tensor")
    z = lax.axis_index("dp")
    docs, width = N * DOCS_DEV, OWN * RANK
    sketch_ref[...] = col_ref[z]
    cols = col_ref[...].reshape(docs, width)
    rows = jnp.where(q == z, cols, row_ref[...].reshape(docs, width))
    col_hi, col_lo = split(cols)
    row_hi, row_lo = split(rows.T)
    lhs = jnp.concatenate([row_hi, row_lo, row_hi], axis=1)
    rhs = jnp.concatenate([col_hi, col_hi, col_lo], axis=0)
    fisher_ref[...] = jnp.dot(lhs, rhs, preferred_element_type=F32) * (1.0 / docs)


def per_device_fused(activations, out_grads, proj_in, proj_out, document_ids):
    tokens, ff = activations.shape
    width = out_grads.shape[1]
    blocks = tokens // TB
    ids = document_ids.reshape(blocks, 1, TB)
    vmem = pl.BlockSpec(memory_space=pltpu.VMEM)
    hbm = pl.BlockSpec(memory_space=pl.ANY)
    cols = OWN * RANK
    dma = pltpu.SemaphoreType.DMA
    gathered = jax.ShapeDtypeStruct((N, DOCS_DEV, cols), F32)
    scol, srow = pl.pallas_call(
        kernel,
        out_shape=(gathered, gathered),
        in_specs=[hbm, hbm, hbm, hbm, vmem],
        out_specs=(hbm, hbm),
        scratch_shapes=[
            pltpu.VMEM((blocks, TB, ff), BF16),
            pltpu.VMEM((blocks, TB, width), BF16),
            pltpu.VMEM((RANK, ff), BF16),
            pltpu.VMEM((RANK, width), BF16),
            pltpu.VMEM((blocks, 2 * RANK, TB), F32),
            pltpu.VMEM((blocks, 2 * RANK, TB), F32),
            pltpu.VMEM((blocks, RANK + OWN, TB), F32),
            pltpu.VMEM((blocks, RANK + OWN, TB), F32),
            pltpu.VMEM((blocks, RANK + OWN, TB), F32),
            pltpu.VMEM((2 * OWN * DOCS_DEV, 2 * RANK), F32),
            pltpu.VMEM((DOCS_DEV, TB), F32),
            pltpu.VMEM((DOCS_DEV, cols), F32),
            dma((blocks,)), dma((blocks,)), dma((2,)), dma((blocks,)), dma((blocks,)),
            dma((blocks,)), dma((blocks,)),
            dma, dma((N - 1,)), dma((N - 1,)), dma((N - 1,)), dma((N,)),
        ],
        compiler_params=pltpu.CompilerParams(
            collective_id=0, has_side_effects=True, vmem_limit_bytes=58 * 1024 * 1024
        ),
        cost_estimate=pl.CostEstimate(
            flops=2 * tokens * (ff + width) * RANK,
            bytes_accessed=2 * tokens * (ff + width), transcendentals=0,
        ),
    )(activations, out_grads, proj_in.T, proj_out.T, ids)
    return pl.pallas_call(
        fisher_kernel,
        out_shape=(
            jax.ShapeDtypeStruct((DOCS_DEV, cols), F32),
            jax.ShapeDtypeStruct((cols, cols), F32),
        ),
        in_specs=[vmem, vmem],
        out_specs=(vmem, vmem),
    )(scol, srow)


def solution(mesh):
    fits = mesh.shape["tensor"] == N and mesh.shape["dp"] == N
    return jax.shard_map(
        per_device_fused if fits else per_device_general,
        mesh=mesh,
        in_specs=(
            P(("groups", "dp"), "tensor"),
            P(("groups", "dp"), "tensor"),
            P(("groups", "tensor"), None),
            P(("groups", "tensor"), None),
            P(("groups", "dp"), None),
        ),
        out_specs=(P(("groups", "dp"), "tensor"), P(("groups", "dp"), "tensor")),
        check_vma=False,
    )
```

```python
import jax
import jax.numpy as jnp
from jax import lax
from jax.experimental import pallas as pl
from jax.experimental.pallas import tpu as pltpu
from jax.sharding import PartitionSpec as P

DOCS_DEV = 32
MESH = pl.DeviceIdType.MESH
F32 = jnp.float32
BF16 = jnp.bfloat16


def sketch_terms(in_proj, out_proj, weighted):
    token_count = in_proj.shape[0]
    rank_size = in_proj.shape[1]
    outer_rows = (out_proj[:, :, None] * in_proj[:, None, :]).reshape(
        token_count, rank_size * rank_size
    )
    return jnp.dot(weighted.T, outer_rows, precision=lax.Precision.HIGHEST)


def per_device_general(activations, out_grads, proj_in, proj_out, document_ids):
    in_part = jnp.dot(activations, proj_in, preferred_element_type=F32)
    out_part = jnp.dot(out_grads, proj_out, preferred_element_type=F32)
    onehot = (document_ids[0][:, None] == jnp.arange(DOCS_DEV, dtype=jnp.int32)[None, :]).astype(F32)
    length = jnp.sum(onehot, axis=0)
    weighted = onehot * lax.rsqrt(length)[None, :]
    tensor_count = lax.axis_size("tensor")
    tensor_index = lax.axis_index("tensor")
    sketch_size = proj_in.shape[1] * proj_in.shape[1]
    col_count = sketch_size // tensor_count
    in_proj, out_proj = lax.psum((in_part, out_part), "tensor")
    full_sketch = sketch_terms(in_proj, out_proj, weighted)
    own_sketch = lax.dynamic_slice_in_dim(full_sketch, tensor_index * col_count, col_count, 1)
    dp_count = lax.axis_size("dp")
    block_rows = sketch_size // dp_count
    row_first = lax.axis_index("dp") * block_rows
    rows_piece = lax.dynamic_slice_in_dim(
        lax.all_gather(full_sketch, "dp", axis=0, tiled=True), row_first, block_rows, 1
    )
    cols_piece = lax.all_gather(own_sketch, "dp", axis=0, tiled=True)
    fisher = jnp.dot(rows_piece.T, cols_piece, precision=lax.Precision.HIGHEST)
    return (own_sketch, fisher / (DOCS_DEV * dp_count))


N = 4
TB = 512
MOST = 128
EARLY = 8
RANK = 32
OWN = RANK // N


def split(x):
    hi = x.astype(BF16)
    return hi, (x - hi.astype(F32)).astype(BF16)


def across(a, b):
    return lax.dot_general(a, b, (((1,), (1,)), ((), ())), preferred_element_type=F32)


def kernel(
    act_hbm, grad_hbm, pin_hbm, pout_hbm, ids_ref, scol, srow,
    act, grad, pin_ref, pout_ref, part, sib, mine, send, recv, acc, count, own,
    act_sem, grad_sem, proj_sem, sib_send, sib_recv, x_send, x_recv,
    own_sem, col_send, col_recv, row_send, row_recv,
):
    q = lax.axis_index("tensor")
    z = lax.axis_index("dp")
    blocks = act.shape[0]
    core_peer = q + 1 - 2 * lax.rem(q, 2)
    chip_peer = lax.rem(q + 2, N)

    def load(b):
        rows = pl.ds(pl.multiple_of(b * TB, TB), TB)
        return (
            pltpu.make_async_copy(grad_hbm.at[rows], grad.at[b], grad_sem.at[b]),
            pltpu.make_async_copy(act_hbm.at[rows], act.at[b], act_sem.at[b]),
        )

    def to_core(b):
        return pltpu.make_async_remote_copy(
            src_ref=part.at[b], dst_ref=sib.at[b], send_sem=sib_send.at[b], recv_sem=sib_recv.at[b],
            device_id={"tensor": core_peer}, device_id_type=MESH,
        )

    def to_chip(b):
        return pltpu.make_async_remote_copy(
            src_ref=send.at[b], dst_ref=recv.at[b], send_sem=x_send.at[b], recv_sem=x_recv.at[b],
            device_id={"tensor": chip_peer}, device_id_type=MESH,
        )

    proj_copies = (
        pltpu.make_async_copy(pout_hbm, pout_ref, proj_sem.at[0]),
        pltpu.make_async_copy(pin_hbm, pin_ref, proj_sem.at[1]),
    )
    for copy in proj_copies:
        copy.start()

    @pl.loop(0, blocks)
    def _(b):
        for copy in load(b):
            copy.start()

    barrier = pltpu.get_barrier_semaphore()
    for dq in range(N):
        for dz in range(N):
            if dq or dz:
                pl.semaphore_signal(
                    barrier, inc=1,
                    device_id={"tensor": lax.rem(q + dq, N), "dp": lax.rem(z + dz, N)},
                    device_id_type=MESH,
                )

    acc[...] = jnp.zeros_like(acc)
    docs = lax.broadcasted_iota(jnp.int32, (DOCS_DEV, 1), 0)
    count[...] = jnp.zeros_like(count)

    def project(b):
        grad_copy, act_copy = load(b)
        grad_copy.wait()
        act_copy.wait()
        part[b, pl.ds(RANK, RANK)] = across(pout_ref[...], grad[b])
        part[b, pl.ds(0, RANK)] = across(pin_ref[...], act[b])

        @pl.when(b == 0)
        def _():
            pl.semaphore_wait(barrier, N * N - 1)

        to_core(b).start()

    def chip_sum(b):
        to_core(b).wait()
        total = part[b, pl.ds(0, RANK)] + sib[b, pl.ds(0, RANK)]
        mine[b, pl.ds(0, RANK)] = total
        send[b, pl.ds(0, RANK)] = total
        here = pl.ds(pl.multiple_of(RANK + q * OWN, OWN), OWN)
        there = pl.ds(pl.multiple_of(RANK + chip_peer * OWN, OWN), OWN)
        mine[b, pl.ds(RANK, OWN)] = part[b, here] + sib[b, here]
        send[b, pl.ds(RANK, OWN)] = part[b, there] + sib[b, there]
        to_chip(b).start()

    def sketch(b):
        to_chip(b).wait()
        total = mine[b] + recv[b]
        in_hi, in_lo = split(total[:RANK])
        rhs = jnp.concatenate([in_hi, in_lo], axis=0)
        same = (ids_ref[b] == docs).astype(F32)
        count[...] += same
        out = total[RANK:]
        out_hi = out.astype(BF16).astype(F32)
        out_lo = out - out_hi
        rows = [same * o[i : i + 1] for o in (out_hi, out_lo) for i in range(OWN)]
        lhs = jnp.concatenate(rows, axis=0).astype(BF16)
        acc[...] += across(lhs, rhs)

    for copy in proj_copies:
        copy.wait()

    parts = ((0, EARLY), (EARLY, DOCS_DEV - EARLY))

    def finish(p):
        first, size = parts[p]
        half = OWN * DOCS_DEV
        scale = lax.rsqrt(jnp.sum(count[pl.ds(first, size)], axis=1, keepdims=True))
        for i in range(OWN):
            hi = acc[pl.ds(i * DOCS_DEV + first, size)]
            lo = acc[pl.ds(half + i * DOCS_DEV + first, size)]
            both = hi + lo
            piece = (both[:, :RANK] + both[:, RANK:]) * scale
            own[pl.ds(first, size), pl.ds(i * RANK, RANK)] = piece
        for d in range(N - 1):
            col_copy(p, (1, 0, 2)[d], z).start()
            row_copy(p, d, z).start()

    def col_copy(p, d, slot):
        return pltpu.make_async_remote_copy(
            src_ref=own.at[pl.ds(*parts[p])], dst_ref=scol.at[slot, pl.ds(*parts[p])],
            send_sem=col_send.at[p, d], recv_sem=col_recv.at[p, d],
            device_id={"dp": lax.rem(z + d + 1, N)}, device_id_type=MESH,
        )

    def row_copy(p, d, slot):
        return pltpu.make_async_remote_copy(
            src_ref=own.at[pl.ds(*parts[p])], dst_ref=srow.at[slot, pl.ds(*parts[p])],
            send_sem=row_send.at[p, d], recv_sem=row_recv.at[p, slot],
            device_id={"tensor": lax.rem(q + d + 1, N), "dp": q}, device_id_type=MESH,
        )

    @pl.loop(0, blocks + 2)
    def _(b):
        pl.when(b < blocks)(lambda: project(b))
        pl.when((b > 0) & (b <= blocks))(lambda: chip_sum(b - 1))
        pl.when(b > 1)(lambda: sketch(b - 2))
        pl.when(b == EARLY * MOST // TB + 1)(lambda: finish(0))

    finish(1)
    keep = pltpu.make_async_copy(own, scol.at[z], own_sem)
    keep.start()
    keep.wait()
    for p in range(2):
        for d in range(N - 1):
            col_copy(p, d, lax.rem(z + N - d - 1, N)).wait_recv()

    @pl.when(q != z)
    def _():
        for p in range(2):
            for d in range(N):
                row_copy(p, 0, d).wait_recv()

    for p in range(2):
        for d in range(N - 1):
            row_copy(p, d, z).wait_send()
            col_copy(p, d, z).wait_send()


def fisher_kernel(col_ref, row_ref, sketch_ref, fisher_ref):
    q = lax.axis_index("tensor")
    z = lax.axis_index("dp")
    docs, width = N * DOCS_DEV, OWN * RANK
    sketch_ref[...] = col_ref[z]
    cols = col_ref[...].reshape(docs, width)
    rows = jnp.where(q == z, cols, row_ref[...].reshape(docs, width))
    col_hi, col_lo = split(cols)
    row_hi, row_lo = split(rows.T)
    lhs = jnp.concatenate([row_hi, row_lo, row_hi], axis=1)
    rhs = jnp.concatenate([col_hi, col_hi, col_lo], axis=0)
    fisher_ref[...] = jnp.dot(lhs, rhs, preferred_element_type=F32) * (1.0 / docs)


def per_device_fused(activations, out_grads, proj_in, proj_out, document_ids):
    tokens, ff = activations.shape
    width = out_grads.shape[1]
    blocks = tokens // TB
    ids = document_ids.reshape(blocks, 1, TB)
    vmem = pl.BlockSpec(memory_space=pltpu.VMEM)
    hbm = pl.BlockSpec(memory_space=pl.ANY)
    cols = OWN * RANK
    dma = pltpu.SemaphoreType.DMA
    gathered = jax.ShapeDtypeStruct((N, DOCS_DEV, cols), F32)
    scol, srow = pl.pallas_call(
        kernel,
        out_shape=(gathered, gathered),
        in_specs=[hbm, hbm, hbm, hbm, vmem],
        out_specs=(hbm, hbm),
        scratch_shapes=[
            pltpu.VMEM((blocks, TB, ff), BF16),
            pltpu.VMEM((blocks, TB, width), BF16),
            pltpu.VMEM((RANK, ff), BF16),
            pltpu.VMEM((RANK, width), BF16),
            pltpu.VMEM((blocks, 2 * RANK, TB), F32),
            pltpu.VMEM((blocks, 2 * RANK, TB), F32),
            pltpu.VMEM((blocks, RANK + OWN, TB), F32),
            pltpu.VMEM((blocks, RANK + OWN, TB), F32),
            pltpu.VMEM((blocks, RANK + OWN, TB), F32),
            pltpu.VMEM((2 * OWN * DOCS_DEV, 2 * RANK), F32),
            pltpu.VMEM((DOCS_DEV, TB), F32),
            pltpu.VMEM((DOCS_DEV, cols), F32),
            dma((blocks,)), dma((blocks,)), dma((2,)), dma((blocks,)), dma((blocks,)),
            dma((blocks,)), dma((blocks,)),
            dma, dma((2, N - 1)), dma((2, N - 1)), dma((2, N - 1)), dma((2, N)),
        ],
        compiler_params=pltpu.CompilerParams(
            collective_id=0, has_side_effects=True, vmem_limit_bytes=58 * 1024 * 1024
        ),
        cost_estimate=pl.CostEstimate(
            flops=2 * tokens * (ff + width) * RANK,
            bytes_accessed=2 * tokens * (ff + width), transcendentals=0,
        ),
    )(activations, out_grads, proj_in.T, proj_out.T, ids)
    return pl.pallas_call(
        fisher_kernel,
        out_shape=(
            jax.ShapeDtypeStruct((DOCS_DEV, cols), F32),
            jax.ShapeDtypeStruct((cols, cols), F32),
        ),
        in_specs=[vmem, vmem],
        out_specs=(vmem, vmem),
    )(scol, srow)


def solution(mesh):
    fits = mesh.shape["tensor"] == N and mesh.shape["dp"] == N
    return jax.shard_map(
        per_device_fused if fits else per_device_general,
        mesh=mesh,
        in_specs=(
            P(("groups", "dp"), "tensor"),
            P(("groups", "dp"), "tensor"),
            P(("groups", "tensor"), None),
            P(("groups", "tensor"), None),
            P(("groups", "dp"), None),
        ),
        out_specs=(P(("groups", "dp"), "tensor"), P(("groups", "dp"), "tensor")),
        check_vma=False,
    )
```

```python
import jax
import jax.numpy as jnp
from jax import lax
from jax.experimental import pallas as pl
from jax.experimental.pallas import tpu as pltpu
from jax.sharding import PartitionSpec as P

DOCS_DEV = 32
MESH = pl.DeviceIdType.MESH
F32 = jnp.float32
BF16 = jnp.bfloat16


def sketch_terms(in_proj, out_proj, weighted):
    token_count = in_proj.shape[0]
    rank_size = in_proj.shape[1]
    outer_rows = (out_proj[:, :, None] * in_proj[:, None, :]).reshape(
        token_count, rank_size * rank_size
    )
    return jnp.dot(weighted.T, outer_rows, precision=lax.Precision.HIGHEST)


def per_device_general(activations, out_grads, proj_in, proj_out, document_ids):
    in_part = jnp.dot(activations, proj_in, preferred_element_type=F32)
    out_part = jnp.dot(out_grads, proj_out, preferred_element_type=F32)
    onehot = (document_ids[0][:, None] == jnp.arange(DOCS_DEV, dtype=jnp.int32)[None, :]).astype(F32)
    length = jnp.sum(onehot, axis=0)
    weighted = onehot * lax.rsqrt(length)[None, :]
    tensor_count = lax.axis_size("tensor")
    tensor_index = lax.axis_index("tensor")
    sketch_size = proj_in.shape[1] * proj_in.shape[1]
    col_count = sketch_size // tensor_count
    in_proj, out_proj = lax.psum((in_part, out_part), "tensor")
    full_sketch = sketch_terms(in_proj, out_proj, weighted)
    own_sketch = lax.dynamic_slice_in_dim(full_sketch, tensor_index * col_count, col_count, 1)
    dp_count = lax.axis_size("dp")
    block_rows = sketch_size // dp_count
    row_first = lax.axis_index("dp") * block_rows
    rows_piece = lax.dynamic_slice_in_dim(
        lax.all_gather(full_sketch, "dp", axis=0, tiled=True), row_first, block_rows, 1
    )
    cols_piece = lax.all_gather(own_sketch, "dp", axis=0, tiled=True)
    fisher = jnp.dot(rows_piece.T, cols_piece, precision=lax.Precision.HIGHEST)
    return (own_sketch, fisher / (DOCS_DEV * dp_count))


N = 4
TB = 512
SUB = 256
MOST = 128
EARLY = 8
RANK = 32
OWN = RANK // N


def split(x):
    hi = x.astype(BF16)
    return hi, (x - hi.astype(F32)).astype(BF16)


def across(a, b):
    return lax.dot_general(a, b, (((1,), (1,)), ((), ())), preferred_element_type=F32)


def kernel(
    act_hbm, grad_hbm, pin_hbm, pout_hbm, ids_ref, scol, srow,
    act, grad, pin_ref, pout_ref, part, sib, mine, send, recv, acc, count, own,
    act_sem, grad_sem, proj_sem, sib_send, sib_recv, x_send, x_recv,
    own_sem, col_send, col_recv, row_send, row_recv,
):
    q = lax.axis_index("tensor")
    z = lax.axis_index("dp")
    pieces = act.shape[0]
    blocks = part.shape[0]
    core_peer = q + 1 - 2 * lax.rem(q, 2)
    chip_peer = lax.rem(q + 2, N)

    def load(c):
        rows = pl.ds(pl.multiple_of(c * SUB, SUB), SUB)
        return (
            pltpu.make_async_copy(grad_hbm.at[rows], grad.at[c], grad_sem.at[c]),
            pltpu.make_async_copy(act_hbm.at[rows], act.at[c], act_sem.at[c]),
        )

    def to_core(b):
        return pltpu.make_async_remote_copy(
            src_ref=part.at[b], dst_ref=sib.at[b], send_sem=sib_send.at[b], recv_sem=sib_recv.at[b],
            device_id={"tensor": core_peer}, device_id_type=MESH,
        )

    def to_chip(b):
        return pltpu.make_async_remote_copy(
            src_ref=send.at[b], dst_ref=recv.at[b], send_sem=x_send.at[b], recv_sem=x_recv.at[b],
            device_id={"tensor": chip_peer}, device_id_type=MESH,
        )

    proj_copies = (
        pltpu.make_async_copy(pout_hbm, pout_ref, proj_sem.at[0]),
        pltpu.make_async_copy(pin_hbm, pin_ref, proj_sem.at[1]),
    )
    for copy in proj_copies:
        copy.start()

    @pl.loop(0, pieces)
    def _(c):
        for copy in load(c):
            copy.start()

    barrier = pltpu.get_barrier_semaphore()
    for dq in range(N):
        for dz in range(N):
            if dq or dz:
                pl.semaphore_signal(
                    barrier, inc=1,
                    device_id={"tensor": lax.rem(q + dq, N), "dp": lax.rem(z + dz, N)},
                    device_id_type=MESH,
                )

    acc[...] = jnp.zeros_like(acc)
    docs = lax.broadcasted_iota(jnp.int32, (DOCS_DEV, 1), 0)
    count[...] = jnp.zeros_like(count)

    def project(b):
        @pl.loop(0, TB // SUB)
        def _(h):
            c = b * (TB // SUB) + h
            at = pl.ds(pl.multiple_of(h * SUB, SUB), SUB)
            for copy in load(c):
                copy.wait()
            part[b, pl.ds(RANK, RANK), at] = across(pout_ref[...], grad[c])
            part[b, pl.ds(0, RANK), at] = across(pin_ref[...], act[c])

        @pl.when(b == 0)
        def _():
            pl.semaphore_wait(barrier, N * N - 1)

        to_core(b).start()

    def chip_sum(b):
        to_core(b).wait()
        total = part[b, pl.ds(0, RANK)] + sib[b, pl.ds(0, RANK)]
        mine[b, pl.ds(0, RANK)] = total
        send[b, pl.ds(0, RANK)] = total
        here = pl.ds(pl.multiple_of(RANK + q * OWN, OWN), OWN)
        there = pl.ds(pl.multiple_of(RANK + chip_peer * OWN, OWN), OWN)
        mine[b, pl.ds(RANK, OWN)] = part[b, here] + sib[b, here]
        send[b, pl.ds(RANK, OWN)] = part[b, there] + sib[b, there]
        to_chip(b).start()

    def sketch(b):
        to_chip(b).wait()
        total = mine[b] + recv[b]
        in_hi, in_lo = split(total[:RANK])
        rhs = jnp.concatenate([in_hi, in_lo], axis=0)
        same = (ids_ref[b] == docs).astype(F32)
        count[...] += same
        out = total[RANK:]
        out_hi = out.astype(BF16).astype(F32)
        out_lo = out - out_hi
        rows = [same * o[i : i + 1] for o in (out_hi, out_lo) for i in range(OWN)]
        lhs = jnp.concatenate(rows, axis=0).astype(BF16)
        acc[...] += across(lhs, rhs)

    for copy in proj_copies:
        copy.wait()

    parts = ((0, EARLY), (EARLY, DOCS_DEV - EARLY))

    def finish(p):
        first, size = parts[p]
        half = OWN * DOCS_DEV
        scale = lax.rsqrt(jnp.sum(count[pl.ds(first, size)], axis=1, keepdims=True))
        for i in range(OWN):
            hi = acc[pl.ds(i * DOCS_DEV + first, size)]
            lo = acc[pl.ds(half + i * DOCS_DEV + first, size)]
            both = hi + lo
            piece = (both[:, :RANK] + both[:, RANK:]) * scale
            own[pl.ds(first, size), pl.ds(i * RANK, RANK)] = piece
        for d in range(N - 1):
            col_copy(p, (1, 0, 2)[d], z).start()
            row_copy(p, d, z).start()

    def col_copy(p, d, slot):
        return pltpu.make_async_remote_copy(
            src_ref=own.at[pl.ds(*parts[p])], dst_ref=scol.at[slot, pl.ds(*parts[p])],
            send_sem=col_send.at[p, d], recv_sem=col_recv.at[p, d],
            device_id={"dp": lax.rem(z + d + 1, N)}, device_id_type=MESH,
        )

    def row_copy(p, d, slot):
        return pltpu.make_async_remote_copy(
            src_ref=own.at[pl.ds(*parts[p])], dst_ref=srow.at[slot, pl.ds(*parts[p])],
            send_sem=row_send.at[p, d], recv_sem=row_recv.at[p, slot],
            device_id={"tensor": lax.rem(q + d + 1, N), "dp": q}, device_id_type=MESH,
        )

    @pl.loop(0, blocks + 2)
    def _(b):
        pl.when(b < blocks)(lambda: project(b))
        pl.when((b > 0) & (b <= blocks))(lambda: chip_sum(b - 1))
        pl.when(b > 1)(lambda: sketch(b - 2))
        pl.when(b == EARLY * MOST // TB + 1)(lambda: finish(0))

    finish(1)
    keep = pltpu.make_async_copy(own, scol.at[z], own_sem)
    keep.start()
    keep.wait()
    for p in range(2):
        for d in range(N - 1):
            col_copy(p, d, lax.rem(z + N - d - 1, N)).wait_recv()

    @pl.when(q != z)
    def _():
        for p in range(2):
            for d in range(N):
                row_copy(p, 0, d).wait_recv()

    for p in range(2):
        for d in range(N - 1):
            row_copy(p, d, z).wait_send()
            col_copy(p, d, z).wait_send()


def fisher_kernel(col_ref, row_ref, sketch_ref, fisher_ref):
    q = lax.axis_index("tensor")
    z = lax.axis_index("dp")
    docs, width = N * DOCS_DEV, OWN * RANK
    sketch_ref[...] = col_ref[z]
    cols = col_ref[...].reshape(docs, width)
    rows = jnp.where(q == z, cols, row_ref[...].reshape(docs, width))
    col_hi, col_lo = split(cols)
    row_hi, row_lo = split(rows.T)
    lhs = jnp.concatenate([row_hi, row_lo, row_hi], axis=1)
    rhs = jnp.concatenate([col_hi, col_hi, col_lo], axis=0)
    fisher_ref[...] = jnp.dot(lhs, rhs, preferred_element_type=F32) * (1.0 / docs)


def per_device_fused(activations, out_grads, proj_in, proj_out, document_ids):
    tokens, ff = activations.shape
    width = out_grads.shape[1]
    blocks = tokens // TB
    ids = document_ids.reshape(blocks, 1, TB)
    vmem = pl.BlockSpec(memory_space=pltpu.VMEM)
    hbm = pl.BlockSpec(memory_space=pl.ANY)
    cols = OWN * RANK
    dma = pltpu.SemaphoreType.DMA
    gathered = jax.ShapeDtypeStruct((N, DOCS_DEV, cols), F32)
    scol, srow = pl.pallas_call(
        kernel,
        out_shape=(gathered, gathered),
        in_specs=[hbm, hbm, hbm, hbm, vmem],
        out_specs=(hbm, hbm),
        scratch_shapes=[
            pltpu.VMEM((tokens // SUB, SUB, ff), BF16),
            pltpu.VMEM((tokens // SUB, SUB, width), BF16),
            pltpu.VMEM((RANK, ff), BF16),
            pltpu.VMEM((RANK, width), BF16),
            pltpu.VMEM((blocks, 2 * RANK, TB), F32),
            pltpu.VMEM((blocks, 2 * RANK, TB), F32),
            pltpu.VMEM((blocks, RANK + OWN, TB), F32),
            pltpu.VMEM((blocks, RANK + OWN, TB), F32),
            pltpu.VMEM((blocks, RANK + OWN, TB), F32),
            pltpu.VMEM((2 * OWN * DOCS_DEV, 2 * RANK), F32),
            pltpu.VMEM((DOCS_DEV, TB), F32),
            pltpu.VMEM((DOCS_DEV, cols), F32),
            dma((tokens // SUB,)), dma((tokens // SUB,)), dma((2,)), dma((blocks,)), dma((blocks,)),
            dma((blocks,)), dma((blocks,)),
            dma, dma((2, N - 1)), dma((2, N - 1)), dma((2, N - 1)), dma((2, N)),
        ],
        compiler_params=pltpu.CompilerParams(
            collective_id=0, has_side_effects=True, vmem_limit_bytes=58 * 1024 * 1024
        ),
        cost_estimate=pl.CostEstimate(
            flops=2 * tokens * (ff + width) * RANK,
            bytes_accessed=2 * tokens * (ff + width), transcendentals=0,
        ),
    )(activations, out_grads, proj_in.T, proj_out.T, ids)
    return pl.pallas_call(
        fisher_kernel,
        out_shape=(
            jax.ShapeDtypeStruct((DOCS_DEV, cols), F32),
            jax.ShapeDtypeStruct((cols, cols), F32),
        ),
        in_specs=[vmem, vmem],
        out_specs=(vmem, vmem),
    )(scol, srow)


def solution(mesh):
    fits = mesh.shape["tensor"] == N and mesh.shape["dp"] == N
    return jax.shard_map(
        per_device_fused if fits else per_device_general,
        mesh=mesh,
        in_specs=(
            P(("groups", "dp"), "tensor"),
            P(("groups", "dp"), "tensor"),
            P(("groups", "tensor"), None),
            P(("groups", "tensor"), None),
            P(("groups", "dp"), None),
        ),
        out_specs=(P(("groups", "dp"), "tensor"), P(("groups", "dp"), "tensor")),
        check_vma=False,
    )
```
